32 devices in a mesh: dom: 8 (over y, x, core), sub: 4 (over z).
Axes of the slice: x: 2, y: 2, z: 4, core: 2. Of those that a mesh axis runs over, the one named last changes fastest.
Arguments:
- adjoint: float32 [3, 128, 96, 128], P(None, 'dom', 'sub'), may hold values from -15 to 15
- base_flow: float32 [3, 128, 96, 128], P(None, 'dom', 'sub'), may hold values from -6 to 6
- stiffness: float32 [128, 96, 128], P('dom', 'sub'), may hold values from 0.5 to 2
- mass_weight: float32 [128, 96, 128], P('dom', 'sub'), may hold values from 0.05 to 0.2
Outputs:
- adjoint_next: float32 [3, 128, 96, 128], P(None, 'dom', 'sub')
The draws below stay inside these ranges and needn't reach their ends.
All inputs are finite; a program needn't handle non-finite values.
Results may differ from the reference program's by a relative error of at most 0.009.
Values sent between devices are 32-bit elements; how exact they have to be, the bound alone decides.
A program may use at most 64 MiB of HBM per device.

```python
import math
import jax
import jax.numpy as jnp
import numpy as np
from jax import lax

ITERS = 2
PR = 128
NX = 128
NY = 96


def ramped_field(noise, top):
    position = jnp.arange(NX).astype(jnp.float32) / float(max(NX - 1, 1))
    ramp = 1.0 + (top - 1.0) * position
    return noise * ramp.reshape((1, NX, 1, 1))


def draw_adjoint(key, part):
    key = jax.random.fold_in(key, 7)
    noise = jnp.clip(jax.random.normal(key, (3, NX, NY, PR), jnp.float32), -6.0, 6.0)
    return ramped_field(noise, 2.5)


def shard_levels(own_key, dims, split, least, largest):
    gain = 1.0
    for dim, parts in split:
        steps = jax.random.uniform(jax.random.fold_in(jax.random.fold_in(own_key, 6), dim), (parts,), jnp.float32, least / len(split), largest / len(split))
        gain = gain * jnp.repeat(jnp.exp(steps), dims[dim] // parts).reshape((-1,) + (1,) * (len(dims) - 1 - dim))
    return gain


def gaussian(own_key, shape, spread, bound, split=(), dtype=jnp.bfloat16):
    values = spread * jax.random.normal(own_key, shape, jnp.float32)
    if split:
        values = values * shard_levels(own_key, shape, split, -0.22, 0.18)
    return jnp.clip(values, -bound, bound).astype(dtype)


def setup_inputs(seed: int = 0) -> dict:
    streams_of = jax.random.split(jax.random.key(seed), 5)
    return {
        "adjoint": draw_adjoint(jax.random.fold_in(streams_of[4], 71), 0),
        "base_flow": gaussian(streams_of[1], (3, NX, NY, PR), 1.0, 6.0, ((1, 8), (2, 4)), jnp.float32),
        "stiffness": jnp.clip(jnp.exp(math.log(2.0) - 1.3862944 * jax.random.uniform(streams_of[2], (NX, NY, PR), jnp.float32) ** shard_levels(streams_of[2], (NX, NY, PR), ((0, 8), (1, 4)), -0.2, 0.2)), 0.5, 2.0),
        "mass_weight": jnp.clip(jnp.exp(math.log(0.2) - 1.3862944 * jax.random.uniform(streams_of[3], (NX, NY, PR), jnp.float32) ** shard_levels(streams_of[3], (NX, NY, PR), ((0, 8), (1, 4)), -0.2, 0.2)), 0.05, 0.2),
    }


shift_mass = 100.0


def legendre_seven(points):
    previous = np.ones(points.shape)
    current = points * 1.0
    for order in range(1, 7):
        following = ((2 * order + 1) * points * current - order * previous) / (order + 1)
        previous = current
        current = following
    return current


def derivative_table():
    degree = 7
    abscissae = np.array([-1.0, -0.871740148509607, -0.591700181433142, -0.209299217902479, 0.209299217902479, 0.591700181433142, 0.871740148509607, 1.0])
    legendre_values = legendre_seven(abscissae)
    deriv_table = np.zeros((degree + 1, degree + 1))
    for first_index in range(degree + 1):
        for second_index in range(degree + 1):
            if first_index != second_index:
                deriv_table[first_index, second_index] = legendre_values[first_index] / (legendre_values[second_index] * (abscissae[first_index] - abscissae[second_index]))
    deriv_table[0, 0] = -degree * (degree + 1) / 4.0
    deriv_table[degree, degree] = degree * (degree + 1) / 4.0
    return deriv_table


def derive(grid_field, deriv_table, dim_index, transpose):
    axis_index = grid_field.ndim - 3 + dim_index
    dims_shape = grid_field.shape
    split_shape = dims_shape[:axis_index] + (dims_shape[axis_index] // 8, 8) + dims_shape[axis_index + 1:]
    moved_field = jnp.moveaxis(grid_field.reshape(split_shape), axis_index + 1, -1)
    use_matrix = deriv_table if transpose else deriv_table.T
    product = jnp.matmul(moved_field, use_matrix, precision=lax.Precision.HIGHEST)
    return jnp.moveaxis(product, -1, axis_index + 1).reshape(dims_shape)


def seam_pair(length, dim_index, walls):
    position = jnp.arange(length)
    head_mask = position % 8 == 0
    tail_mask = position % 8 == 7
    if walls:
        head_mask = head_mask & (position > 0)
        tail_mask = tail_mask & (position < length - 1)
    view_shape = [1, 1, 1]
    view_shape[dim_index] = length
    return head_mask.astype(jnp.float32).reshape(view_shape), tail_mask.astype(jnp.float32).reshape(view_shape)


def wall_mask(length):
    position = jnp.arange(length)
    return ((position > 0) & (position < length - 1)).astype(jnp.float32).reshape((1, 1, length))


def assemble(grid_field):
    for dim_index in range(3):
        head_mask, tail_mask = seam_pair(grid_field.shape[dim_index - 3], dim_index, dim_index == 2)
        grid_field = grid_field + tail_mask * jnp.roll(grid_field, -1, dim_index - 3) + head_mask * jnp.roll(grid_field, 1, dim_index - 3)
    return grid_field * wall_mask(grid_field.shape[-1])


def node_weights(sizes_three):
    multiple = jnp.ones((1, 1, 1), jnp.float32)
    for dim_index in range(3):
        head_mask, tail_mask = seam_pair(sizes_three[dim_index], dim_index, dim_index == 2)
        multiple = multiple * (1.0 + head_mask + tail_mask)
    return wall_mask(sizes_three[2]) / multiple


def operate(grid_field, stiffness, mass_weight, deriv_table):
    element_sum = shift_mass * mass_weight * grid_field
    for dim_index in range(3):
        element_sum = element_sum + derive(stiffness * derive(grid_field, deriv_table, dim_index, False), deriv_table, dim_index, True)
    return assemble(element_sum)


def conjugate(right_side, stiffness, mass_weight, deriv_table, weight):
    solution = jnp.zeros_like(right_side)
    residual = right_side
    direction = right_side
    norm_now = jnp.sum(residual * residual * weight)
    for iteration in range(ITERS):
        operator_image = operate(direction, stiffness, mass_weight, deriv_table)
        step_length = norm_now / jnp.sum(direction * operator_image * weight)
        solution = solution + step_length * direction
        residual = residual - step_length * operator_image
        if iteration + 1 < ITERS:
            norm_next = jnp.sum(residual * residual * weight)
            direction = residual + (norm_next / norm_now) * direction
            norm_now = norm_next
    return solution


def reference(adjoint, base_flow, stiffness, mass_weight):
    deriv_table = jnp.asarray(derivative_table(), jnp.float32)
    advect = jnp.zeros_like(adjoint)
    transport_list = []
    for dim_index in range(3):
        grad_adjoint = derive(adjoint, deriv_table, dim_index, False)
        advect = advect + base_flow[dim_index] * grad_adjoint
        grad_base = derive(base_flow, deriv_table, dim_index, False)
        transport_list.append(jnp.sum(adjoint * grad_base, axis=0))
    transport = jnp.stack(transport_list)
    right_side = assemble(mass_weight * (shift_mass * adjoint + advect - transport))
    weight = node_weights(stiffness.shape)
    results = []
    for component in range(3):
        results.append(conjugate(right_side[component], stiffness, mass_weight, deriv_table, weight))
    return jnp.stack(results)
```

```python
import functools

import jax
import jax.numpy as jnp
import ml_dtypes
import numpy as np
from jax import lax
from jax.experimental import pallas as pl
from jax.experimental.pallas import tpu as pltpu
from jax.sharding import PartitionSpec as P

MESH = pl.DeviceIdType.MESH
shift_mass = 100.0

DIRECTIONS = ((1, 0), (-1, 0), (0, 1), (0, -1), (1, 1), (1, -1), (-1, 1), (-1, -1))


def legendre_seven(points):
    previous = np.ones(points.shape)
    current = points * 1.0
    for order in range(1, 7):
        following = ((2 * order + 1) * points * current - order * previous) / (order + 1)
        previous = current
        current = following
    return current


def derivative_table():
    degree = 7
    abscissae = np.array(
        [
            -1.0,
            -0.871740148509607,
            -0.591700181433142,
            -0.209299217902479,
            0.209299217902479,
            0.591700181433142,
            0.871740148509607,
            1.0,
        ]
    )
    legendre_values = legendre_seven(abscissae)
    deriv_table = np.zeros((degree + 1, degree + 1))
    for first_index in range(degree + 1):
        for second_index in range(degree + 1):
            if first_index != second_index:
                deriv_table[first_index, second_index] = legendre_values[first_index] / (
                    legendre_values[second_index]
                    * (abscissae[first_index] - abscissae[second_index])
                )
    deriv_table[0, 0] = -degree * (degree + 1) / 4.0
    deriv_table[degree, degree] = degree * (degree + 1) / 4.0
    return deriv_table


TABLE = derivative_table()


def apply_table(matrix, values):
    even = [values[j] + values[7 - j] for j in range(4)]
    odd = [values[j] - values[7 - j] for j in range(4)]
    result = [None] * 8
    for i in range(4):
        p = q = None
        for j in range(4):
            a = float((matrix[i, j] + matrix[i, 7 - j]) / 2)
            b = float((matrix[i, j] - matrix[i, 7 - j]) / 2)
            p = a * even[j] if p is None else p + a * even[j]
            q = b * odd[j] if q is None else q + b * odd[j]
        result[i] = q + p
        result[7 - i] = q - p
    return result


def split_weights(matrix):
    wide = matrix.astype(np.float32)
    high = wide.astype(ml_dtypes.bfloat16)
    low = (wide - high.astype(np.float32)).astype(high.dtype)
    return np.block([[high, low], [high, np.zeros_like(low)]])


def times_weights(rows, weights):
    high = rows.astype(jnp.bfloat16)
    low = (rows - high.astype(jnp.float32)).astype(jnp.bfloat16)
    both = jnp.concatenate([high, low], axis=1)
    product = jnp.dot(both, weights, preferred_element_type=jnp.float32)
    half = rows.shape[1]
    return product[:, :half] + product[:, half:]


def fold8(values):
    total = values[0:8]
    for start in range(8, values.shape[0], 8):
        total = total + values[start : start + 8]
    return total


def kernel(
    sizes,
    adjoint_hbm,
    base_hbm,
    stiff_hbm,
    mass_hbm,
    wd_ref,
    wt_ref,
    out_ref,
    adj,
    base,
    stiff,
    mass,
    u0,
    u1,
    bf,
    qf,
    tmp,
    sy,
    sc,
    rx,
    ry,
    rc,
    dots_send,
    dots_recv,
    load_sem,
    send_sem,
    recv_sem,
    dot_send_sem,
    dot_recv_sem,
):
    nd, ns, nx, ny, nr = sizes
    plane = nx * ny
    me_d = lax.axis_index("dom")
    me_s = lax.axis_index("sub")
    ndev = nd * ns

    loads = []
    for k, (src, dst) in enumerate(
        ((adjoint_hbm, adj), (base_hbm, base), (mass_hbm, mass), (stiff_hbm, stiff))
    ):
        copy = pltpu.make_async_copy(src, dst, load_sem.at[k])
        copy.start()
        loads.append(copy)

    def other(offset):
        flat = lax.rem(me_d * ns + me_s + offset, ndev)
        return (lax.div(flat, ns), lax.rem(flat, ns))

    barrier = pltpu.get_barrier_semaphore()

    @pl.loop(1, ndev)
    def _(offset):
        pl.semaphore_signal(barrier, inc=1, device_id=other(offset), device_id_type=MESH)

    lane = lax.broadcasted_iota(jnp.int32, (1, nr), 1)
    inner = (lane > 0) & (lane < nr - 1)
    head = jnp.where((lane % 8 == 0) & inner, 1.0, 0.0)
    tail = jnp.where((lane % 8 == 7) & inner, 1.0, 0.0)
    wall = jnp.where(inner, 1.0, 0.0)
    lane_weight = wall / (1.0 + head + tail)

    def fold_lanes(v):
        v = v + tail * pltpu.roll(v, nr - 1, 1) + head * pltpu.roll(v, 1, 1)
        return v * wall

    def row(c, x):
        return slice(c * plane + x * ny, c * plane + (x + 1) * ny)

    def across(c, y):
        return pl.ds(c * plane + y, nx, stride=ny)

    def neighbour(k):
        dx, dy = DIRECTIONS[k]
        return (lax.rem(me_d + dx + nd, nd), lax.rem(me_s + dy + ns, ns))

    sent = []

    def halo_copies(p, c, u):
        copies = []
        for k, (dx, dy) in enumerate(DIRECTIONS):
            if dy == 0:
                src = u.at[pl.ds(c * plane + ((nx - 1) * ny if dx > 0 else 0), ny)]
                dst = rx.at[p, c, k]
            elif dx == 0:
                src, dst = sy.at[p, c, k - 2], ry.at[p, c, k - 2]
            else:
                src, dst = sc.at[p, c, k - 4], rc.at[p, c, k - 4]
            copies.append(
                pltpu.make_async_remote_copy(
                    src_ref=src,
                    dst_ref=dst,
                    send_sem=send_sem.at[p, c, k],
                    recv_sem=recv_sem.at[p, c, k],
                    device_id=neighbour(k),
                    device_id_type=MESH,
                )
            )
        return copies

    def send(p, c, u):
        for k in (2, 3):
            y = ny - 1 if k == 2 else 0
            buf = sy.at[p, c, k - 2]
            buf[...] = u[across(c, y), :]
            for e in range(8, nx, 8):
                lo = c * plane + (e - 1) * ny + y
                hi = c * plane + e * ny + y
                both = u[lo : lo + 1, :] + u[hi : hi + 1, :]
                buf[e - 1 : e, :] = both
                buf[e : e + 1, :] = both
        for k in range(4, 8):
            dx, dy = DIRECTIONS[k]
            at = c * plane + ((nx - 1) * ny if dx > 0 else 0) + (ny - 1 if dy > 0 else 0)
            sc[p, c, k - 4] = u[at : at + 1, :]
        copies = halo_copies(p, c, u)
        for copy in copies:
            copy.start()
        sent.append(copies)
        return copies

    def assemble(p, c, u, dst, copies):
        for copy in copies:
            copy.wait_recv()
        for x in range(nx):
            if x == 0:
                v = u[row(c, 0), :] + rx[p, c, 0]
            elif x == nx - 1:
                v = u[row(c, x), :] + rx[p, c, 1]
            elif x % 8 == 7:
                v = u[row(c, x), :] + u[row(c, x + 1), :]
            elif x % 8 == 0:
                v = u[row(c, x), :] + u[row(c, x - 1), :]
            else:
                v = u[row(c, x), :]
            dst[row(c, x), :] = v
        for e in range(8, ny, 8):
            both = dst[across(c, e - 1), :] + dst[across(c, e), :]
            dst[across(c, e - 1), :] = both
            dst[across(c, e), :] = both
        dst[across(c, 0), :] = dst[across(c, 0), :] + ry[p, c, 0]
        dst[across(c, ny - 1), :] = dst[across(c, ny - 1), :] + ry[p, c, 1]
        for k in range(4, 8):
            dx, dy = DIRECTIONS[k]
            at = c * plane + (0 if dx > 0 else (nx - 1) * ny) + (0 if dy > 0 else ny - 1)
            dst[at : at + 1, :] = dst[at : at + 1, :] + rc[p, c, k - 4]

    def x_groups(c, ref):
        for xe in range(0, nx, 8):
            yield xe, [ref[row(c, xe + i), :] for i in range(8)]

    def y_groups(c, ref):
        for ye in range(0, ny, 8):
            yield ye, [ref[across(c, ye + j), :] for j in range(8)]

    for copy in loads[:3]:
        copy.wait()
    halos = []
    for c in range(3):
        part = slice(c * plane, (c + 1) * plane)
        for ye in range(0, ny, 8):
            grads = apply_table(TABLE, [adj[across(c, ye + j), :] for j in range(8)])
            terms = [base[across(1, ye + j), :] * grads[j] for j in range(8)]
            if c == 1:
                for d in range(3):
                    grads = apply_table(TABLE, [base[across(d, ye + j), :] for j in range(8)])
                    terms = [
                        terms[j] - adj[across(d, ye + j), :] * grads[j] for j in range(8)
                    ]
            for j in range(8):
                tmp[across(c, ye + j), :] = terms[j]
        radial = base[2 * plane : 3 * plane, :] * times_weights(adj[part, :], wd_ref[...])
        if c == 2:
            for d in range(3):
                some = slice(d * plane, (d + 1) * plane)
                radial = radial - adj[some, :] * times_weights(base[some, :], wd_ref[...])
        for xe in range(0, nx, 8):
            grads = apply_table(TABLE, [adj[row(c, xe + i), :] for i in range(8)])
            terms = [base[row(0, xe + i), :] * grads[i] for i in range(8)]
            if c == 0:
                for d in range(3):
                    grads = apply_table(TABLE, [base[row(d, xe + i), :] for i in range(8)])
                    terms = [terms[i] - adj[row(d, xe + i), :] * grads[i] for i in range(8)]
            for i in range(8):
                x = xe + i
                total = (
                    shift_mass * adj[row(c, x), :]
                    + terms[i]
                    + tmp[row(c, x), :]
                    + radial[x * ny : (x + 1) * ny]
                )
                u0[row(c, x), :] = fold_lanes(mass[row(0, x), :] * total)
        if c == 0:
            pl.semaphore_wait(barrier, ndev - 1)
        halos.append(send(0, c, u0))

    loads[3].wait()
    table_t = TABLE.T

    dots = [[None] * 4 for _ in range(3)]

    def add(c, k, values):
        values = fold8(values)
        dots[c][k] = values if dots[c][k] is None else dots[c][k] + values

    for c in range(3):
        part = slice(c * plane, (c + 1) * plane)
        assemble(0, c, u0, bf, halos[c])
        radial = stiff[...] * times_weights(bf[part, :], wd_ref[...])
        radial = times_weights(radial, wt_ref[...])
        for ye, values in y_groups(c, bf):
            grads = apply_table(TABLE, values)
            terms = apply_table(
                table_t, [stiff[across(0, ye + j), :] * grads[j] for j in range(8)]
            )
            for j in range(8):
                tmp[across(c, ye + j), :] = terms[j]
        for xe, values in x_groups(c, bf):
            grads = apply_table(TABLE, values)
            terms = apply_table(
                table_t, [stiff[row(0, xe + i), :] * grads[i] for i in range(8)]
            )
            for i in range(8):
                x = xe + i
                total = (
                    shift_mass * mass[row(0, x), :] * values[i]
                    + terms[i]
                    + tmp[row(c, x), :]
                    + radial[x * ny : (x + 1) * ny]
                )
                total = fold_lanes(total)
                u1[row(c, x), :] = total
                add(c, 0, values[i] * u0[row(c, x), :])
                add(c, 1, values[i] * total)
        halos[c] = send(1, c, u1)

    for c in range(3):
        part = slice(c * plane, (c + 1) * plane)
        assemble(1, c, u1, qf, halos[c])
        radial = times_weights(qf[part, :], wd_ref[...])
        add(c, 3, stiff[...] * radial * radial)
        for ye, values in y_groups(c, qf):
            grads = apply_table(TABLE, values)
            for j in range(8):
                add(c, 3, stiff[across(0, ye + j), :] * grads[j] * grads[j])
        for xe, values in x_groups(c, qf):
            grads = apply_table(TABLE, values)
            for i in range(8):
                x = xe + i
                add(c, 2, values[i] * u1[row(c, x), :])
                add(
                    c,
                    3,
                    stiff[row(0, x), :] * grads[i] * grads[i]
                    + shift_mass * mass[row(0, x), :] * values[i] * values[i],
                )

    packed = jnp.zeros((1, nr), jnp.float32)
    for c in range(3):
        for k in range(4):
            line = jnp.sum(dots[c][k], axis=0, keepdims=True)
            if k < 3:
                line = line * lane_weight
            packed = jnp.where(lane == 4 * c + k, jnp.sum(line, axis=1, keepdims=True), packed)
    dots_send[0] = packed

    def dot_copy(offset):
        return pltpu.make_async_remote_copy(
            src_ref=dots_send.at[0],
            dst_ref=dots_recv.at[offset - 1],
            send_sem=dot_send_sem,
            recv_sem=dot_recv_sem,
            device_id=other(offset),
            device_id_type=MESH,
        )

    @pl.loop(1, ndev)
    def _(offset):
        dot_copy(offset).start()

    pltpu.make_async_copy(dots_recv, dots_recv, dot_recv_sem).wait()
    total = packed + jnp.sum(dots_recv[...], axis=0)

    for c in range(3):
        bb, bq, qq, qaq = [total[:, 4 * c + k : 4 * c + k + 1] for k in range(4)]
        step0 = bb / bq
        rr1 = step0 * step0 * qq - bb
        more = 1.0 + rr1 / bb
        curve = more * more * bq - 2.0 * more * step0 * qq + step0 * step0 * qaq
        step1 = rr1 / curve
        on_b = jnp.broadcast_to(step0 + step1 * more, (1, nr))
        on_q = jnp.broadcast_to(step1 * step0, (1, nr))
        part = slice(c * plane, (c + 1) * plane)
        out_ref[part, :] = on_b * bf[part, :] - on_q * qf[part, :]

    for copies in sent:
        for copy in copies:
            copy.wait_send()
    pltpu.make_async_copy(dots_recv, dots_recv, dot_send_sem).wait()


def on_device(nd, ns, adjoint, base_flow, stiffness, mass_weight):
    _, nx, ny, nr = adjoint.shape
    rows = nx * ny
    blocks = np.kron(np.eye(nr // 8), TABLE)
    wd = jnp.asarray(split_weights(blocks.T))
    wt = jnp.asarray(split_weights(blocks))
    f32 = jnp.float32
    vmem = pl.BlockSpec(memory_space=pltpu.VMEM)
    hbm = pl.BlockSpec(memory_space=pl.ANY)
    ndev = nd * ns
    out = pl.pallas_call(
        functools.partial(kernel, (nd, ns, nx, ny, nr)),
        out_shape=jax.ShapeDtypeStruct((3 * rows, nr), f32),
        in_specs=[hbm] * 4 + [vmem] * 2,
        out_specs=vmem,
        scratch_shapes=[
            pltpu.VMEM((3 * rows, nr), f32),
            pltpu.VMEM((3 * rows, nr), f32),
            pltpu.VMEM((rows, nr), f32),
            pltpu.VMEM((rows, nr), f32),
            pltpu.VMEM((3 * rows, nr), f32),
            pltpu.VMEM((3 * rows, nr), f32),
            pltpu.VMEM((3 * rows, nr), f32),
            pltpu.VMEM((3 * rows, nr), f32),
            pltpu.VMEM((3 * rows, nr), f32),
            pltpu.VMEM((2, 3, 2, nx, nr), f32),
            pltpu.VMEM((2, 3, 4, 1, nr), f32),
            pltpu.VMEM((2, 3, 2, ny, nr), f32),
            pltpu.VMEM((2, 3, 2, nx, nr), f32),
            pltpu.VMEM((2, 3, 4, 1, nr), f32),
            pltpu.VMEM((1, 1, nr), f32),
            pltpu.VMEM((ndev - 1, 1, nr), f32),
            pltpu.SemaphoreType.DMA((4,)),
            pltpu.SemaphoreType.DMA((2, 3, 8)),
            pltpu.SemaphoreType.DMA((2, 3, 8)),
            pltpu.SemaphoreType.DMA,
            pltpu.SemaphoreType.DMA,
        ],
        compiler_params=pltpu.CompilerParams(
            collective_id=0, has_side_effects=True, vmem_limit_bytes=32 * 1024 * 1024
        ),
    )(
        adjoint.reshape(3 * rows, nr),
        base_flow.reshape(3 * rows, nr),
        stiffness.reshape(rows, nr),
        mass_weight.reshape(rows, nr),
        wd,
        wt,
    )
    return out.reshape(adjoint.shape)


def solution(mesh):
    in_specs = (
        P(None, "dom", "sub", None),
        P(None, "dom", "sub", None),
        P("dom", "sub", None),
        P("dom", "sub", None),
    )
    out_specs = P(None, "dom", "sub", None)
    return jax.shard_map(
        functools.partial(on_device, mesh.shape["dom"], mesh.shape["sub"]),
        mesh=mesh,
        in_specs=in_specs,
        out_specs=out_specs,
        check_vma=False,
    )
```

```python
import functools

import jax
import jax.numpy as jnp
import ml_dtypes
import numpy as np
from jax import lax
from jax.experimental import pallas as pl
from jax.experimental.pallas import tpu as pltpu
from jax.sharding import PartitionSpec as P

MESH = pl.DeviceIdType.MESH
shift_mass = 100.0
GROUPS = ((0, 1), (1, 1), (2, 1))
VMEM_LIMIT = 63 * 1024 * 1024

DIRECTIONS = ((1, 0), (-1, 0), (0, 1), (0, -1), (1, 1), (1, -1), (-1, 1), (-1, -1))


def legendre_seven(points):
    previous = np.ones(points.shape)
    current = points * 1.0
    for order in range(1, 7):
        following = ((2 * order + 1) * points * current - order * previous) / (order + 1)
        previous = current
        current = following
    return current


def derivative_table():
    degree = 7
    abscissae = np.array(
        [
            -1.0,
            -0.871740148509607,
            -0.591700181433142,
            -0.209299217902479,
            0.209299217902479,
            0.591700181433142,
            0.871740148509607,
            1.0,
        ]
    )
    legendre_values = legendre_seven(abscissae)
    deriv_table = np.zeros((degree + 1, degree + 1))
    for first_index in range(degree + 1):
        for second_index in range(degree + 1):
            if first_index != second_index:
                deriv_table[first_index, second_index] = legendre_values[first_index] / (
                    legendre_values[second_index]
                    * (abscissae[first_index] - abscissae[second_index])
                )
    deriv_table[0, 0] = -degree * (degree + 1) / 4.0
    deriv_table[degree, degree] = degree * (degree + 1) / 4.0
    return deriv_table


TABLE = derivative_table()


def apply_table(matrix, values):
    even = [values[j] + values[7 - j] for j in range(4)]
    odd = [values[j] - values[7 - j] for j in range(4)]
    result = [None] * 8
    for i in range(4):
        p = q = None
        for j in range(4):
            a = float((matrix[i, j] + matrix[i, 7 - j]) / 2)
            b = float((matrix[i, j] - matrix[i, 7 - j]) / 2)
            p = a * even[j] if p is None else p + a * even[j]
            q = b * odd[j] if q is None else q + b * odd[j]
        result[i] = q + p
        result[7 - i] = q - p
    return result


def split_weights(matrix):
    wide = matrix.astype(np.float32)
    high = wide.astype(ml_dtypes.bfloat16)
    low = (wide - high.astype(np.float32)).astype(high.dtype)
    return np.block([[high, low], [high, np.zeros_like(low)]])


def times_weights(rows, weights):
    high = rows.astype(jnp.bfloat16)
    low = (rows - high.astype(jnp.float32)).astype(jnp.bfloat16)
    both = jnp.concatenate([high, low], axis=1)
    product = jnp.dot(both, weights, preferred_element_type=jnp.float32)
    half = rows.shape[1]
    return product[:, :half] + product[:, half:]


def fold8(values):
    total = values[0:8]
    for start in range(8, values.shape[0], 8):
        total = total + values[start : start + 8]
    return total


def kernel(
    sizes,
    adjoint_hbm,
    base_hbm,
    stiff_hbm,
    mass_hbm,
    wd_hbm,
    wt_hbm,
    out_ref,
    adj,
    base,
    stiff,
    mass,
    wd_ref,
    wt_ref,
    u0,
    u1,
    bf,
    qf,
    tmp,
    sy,
    sc,
    rx,
    ry,
    rc,
    dots_send,
    dots_recv,
    load_sem,
    send_sem,
    recv_sem,
    dot_send_sem,
    dot_recv_sem,
):
    nd, ns, nx, ny, nr = sizes
    plane = nx * ny
    me_d = lax.axis_index("dom")
    me_s = lax.axis_index("sub")

    loads = []
    for k, (src, dst) in enumerate(
        (
            (adjoint_hbm, adj),
            (base_hbm, base),
            (mass_hbm, mass),
            (wd_hbm, wd_ref),
            (stiff_hbm, stiff),
            (wt_hbm, wt_ref),
        )
    ):
        copy = pltpu.make_async_copy(src, dst, load_sem.at[k])
        copy.start()
        loads.append(copy)

    def flip(at, mask):
        bit, result = 1, at
        while bit <= mask:
            if mask & bit:
                result = result + bit * (1 - 2 * lax.rem(lax.div(at, bit), 2))
            bit *= 2
        return result

    def hops(k):
        return abs(k % ns) + bin(k // ns // 2).count("1")

    flips_d = [flip(me_d, k) for k in range(nd)]
    flips_s = [flip(me_s, k) for k in range(ns)]
    partners = sorted(range(1, nd * ns), key=hops, reverse=True)

    def partner(k):
        return (flips_d[k // ns], flips_s[k % ns])

    barrier = pltpu.get_barrier_semaphore()

    def greet(device):
        pl.semaphore_signal(barrier, inc=1, device_id=device, device_id_type=MESH)

    for k in partners:
        greet(partner(k))

    lane = lax.broadcasted_iota(jnp.int32, (1, nr), 1)
    inner = (lane > 0) & (lane < nr - 1)
    head = jnp.where((lane % 8 == 0) & inner, 1.0, 0.0)
    tail = jnp.where((lane % 8 == 7) & inner, 1.0, 0.0)
    wall = jnp.where(inner, 1.0, 0.0)
    lane_weight = wall / (1.0 + head + tail)

    def fold_lanes(v):
        v = v + tail * pltpu.roll(v, nr - 1, 1) + head * pltpu.roll(v, 1, 1)
        return v * wall

    def row(c, x):
        return slice(c * plane + x * ny, c * plane + (x + 1) * ny)

    def across(c, y):
        return pl.ds(c * plane + y, nx, stride=ny)

    def neighbour(k):
        dx, dy = DIRECTIONS[k]
        return (lax.rem(me_d + dx + nd, nd), lax.rem(me_s + dy + ns, ns))

    sent = []

    def send(p, c, u):
        for k in (2, 3):
            y = ny - 1 if k == 2 else 0
            buf = sy.at[p, k - 2, c]
            buf[...] = u[c, across(0, y), :]
            for e in range(8, nx, 8):
                lo = (e - 1) * ny + y
                hi = e * ny + y
                both = u[c, lo : lo + 1, :] + u[c, hi : hi + 1, :]
                buf[e - 1 : e, :] = both
                buf[e : e + 1, :] = both
        for k in range(4, 8):
            dx, dy = DIRECTIONS[k]
            at = ((nx - 1) * ny if dx > 0 else 0) + (ny - 1 if dy > 0 else 0)
            sc[p, k - 4, c] = u[c, at : at + 1, :]
        for g, (first, count) in enumerate(GROUPS):
            if c != first + count - 1:
                continue
            some = pl.ds(first, count)
            for k in (4, 5, 6, 7, 0, 1, 2, 3):
                dx, dy = DIRECTIONS[k]
                if dy == 0:
                    src = u.at[some, pl.ds((nx - 1) * ny if dx > 0 else 0, ny)]
                    dst = rx.at[p, k, some]
                elif dx == 0:
                    src, dst = sy.at[p, k - 2, some], ry.at[p, k - 2, some]
                else:
                    src, dst = sc.at[p, k - 4, some], rc.at[p, k - 4, some]
                copy = pltpu.make_async_remote_copy(
                    src_ref=src,
                    dst_ref=dst,
                    send_sem=send_sem.at[p, g, k],
                    recv_sem=recv_sem.at[p, g, k],
                    device_id=neighbour(k),
                    device_id_type=MESH,
                )
                copy.start()
                sent.append((p, first, copy))

    def assemble(p, c, u, dst):
        for phase, first, copy in sent:
            if phase == p and first == c:
                copy.wait_recv()
        for x in range(nx):
            if x == 0:
                v = u[c, row(0, 0), :] + rx[p, 0, c]
            elif x == nx - 1:
                v = u[c, row(0, x), :] + rx[p, 1, c]
            elif x % 8 == 7:
                v = u[c, row(0, x), :] + u[c, row(0, x + 1), :]
            elif x % 8 == 0:
                v = u[c, row(0, x), :] + u[c, row(0, x - 1), :]
            else:
                v = u[c, row(0, x), :]
            dst[row(c, x), :] = v
        for e in range(8, ny, 8):
            both = dst[across(c, e - 1), :] + dst[across(c, e), :]
            dst[across(c, e - 1), :] = both
            dst[across(c, e), :] = both
        dst[across(c, 0), :] = dst[across(c, 0), :] + ry[p, 0, c]
        dst[across(c, ny - 1), :] = dst[across(c, ny - 1), :] + ry[p, 1, c]
        for k in range(4, 8):
            dx, dy = DIRECTIONS[k]
            at = c * plane + (0 if dx > 0 else (nx - 1) * ny) + (0 if dy > 0 else ny - 1)
            dst[at : at + 1, :] = dst[at : at + 1, :] + rc[p, k - 4, c]

    def x_groups(c, ref):
        for xe in range(0, nx, 8):
            yield xe, [ref[row(c, xe + i), :] for i in range(8)]

    def y_groups(c, ref):
        for ye in range(0, ny, 8):
            yield ye, [ref[across(c, ye + j), :] for j in range(8)]

    for copy in loads[:4]:
        copy.wait()
    for c in range(3):
        part = slice(c * plane, (c + 1) * plane)
        for ye in range(0, ny, 8):
            grads = apply_table(TABLE, [adj[across(c, ye + j), :] for j in range(8)])
            terms = [base[across(1, ye + j), :] * grads[j] for j in range(8)]
            if c == 1:
                for d in range(3):
                    grads = apply_table(TABLE, [base[across(d, ye + j), :] for j in range(8)])
                    terms = [
                        terms[j] - adj[across(d, ye + j), :] * grads[j] for j in range(8)
                    ]
            for j in range(8):
                tmp[across(c, ye + j), :] = terms[j]
        radial = base[2 * plane : 3 * plane, :] * times_weights(adj[part, :], wd_ref[...])
        if c == 2:
            for d in range(3):
                some = slice(d * plane, (d + 1) * plane)
                radial = radial - adj[some, :] * times_weights(base[some, :], wd_ref[...])
        for xe in range(0, nx, 8):
            grads = apply_table(TABLE, [adj[row(c, xe + i), :] for i in range(8)])
            terms = [base[row(0, xe + i), :] * grads[i] for i in range(8)]
            if c == 0:
                for d in range(3):
                    grads = apply_table(TABLE, [base[row(d, xe + i), :] for i in range(8)])
                    terms = [terms[i] - adj[row(d, xe + i), :] * grads[i] for i in range(8)]
            for i in range(8):
                x = xe + i
                total = (
                    shift_mass * adj[row(c, x), :]
                    + terms[i]
                    + tmp[row(c, x), :]
                    + radial[x * ny : (x + 1) * ny]
                )
                u0[c, row(0, x), :] = fold_lanes(mass[row(0, x), :] * total)
        if c == 0:
            pl.semaphore_wait(barrier, nd * ns - 1)
        send(0, c, u0)

    for copy in loads[4:]:
        copy.wait()
    table_t = TABLE.T

    dots = [[None] * 4 for _ in range(3)]

    def add(c, k, values):
        values = fold8(values)
        dots[c][k] = values if dots[c][k] is None else dots[c][k] + values

    for c in range(3):
        part = slice(c * plane, (c + 1) * plane)
        assemble(0, c, u0, bf)
        radial = stiff[...] * times_weights(bf[part, :], wd_ref[...])
        radial = times_weights(radial, wt_ref[...])
        for ye, values in y_groups(c, bf):
            grads = apply_table(TABLE, values)
            terms = apply_table(
                table_t, [stiff[across(0, ye + j), :] * grads[j] for j in range(8)]
            )
            for j in range(8):
                tmp[across(c, ye + j), :] = terms[j]
        for xe, values in x_groups(c, bf):
            grads = apply_table(TABLE, values)
            terms = apply_table(
                table_t, [stiff[row(0, xe + i), :] * grads[i] for i in range(8)]
            )
            for i in range(8):
                x = xe + i
                total = (
                    shift_mass * mass[row(0, x), :] * values[i]
                    + terms[i]
                    + tmp[row(c, x), :]
                    + radial[x * ny : (x + 1) * ny]
                )
                total = fold_lanes(total)
                u1[c, row(0, x), :] = total
                add(c, 0, values[i] * u0[c, row(0, x), :])
                add(c, 1, values[i] * total)
        send(1, c, u1)

    for c in range(3):
        part = slice(c * plane, (c + 1) * plane)
        assemble(1, c, u1, qf)
        radial = times_weights(qf[part, :], wd_ref[...])
        add(c, 3, stiff[...] * radial * radial)
        for ye, values in y_groups(c, qf):
            grads = apply_table(TABLE, values)
            for j in range(8):
                add(c, 3, stiff[across(0, ye + j), :] * grads[j] * grads[j])
        for xe, values in x_groups(c, qf):
            grads = apply_table(TABLE, values)
            for i in range(8):
                x = xe + i
                add(c, 2, values[i] * u1[c, row(0, x), :])
                add(
                    c,
                    3,
                    stiff[row(0, x), :] * grads[i] * grads[i]
                    + shift_mass * mass[row(0, x), :] * values[i] * values[i],
                )

    packed = jnp.zeros((1, nr), jnp.float32)
    for c in range(3):
        for k in range(4):
            line = jnp.sum(dots[c][k], axis=0, keepdims=True)
            if k < 3:
                line = line * lane_weight
            packed = jnp.where(lane == 4 * c + k, jnp.sum(line, axis=1, keepdims=True), packed)
    dots_send[0] = packed
    for k in partners:
        pltpu.make_async_remote_copy(
            src_ref=dots_send.at[0],
            dst_ref=dots_recv.at[k - 1],
            send_sem=dot_send_sem,
            recv_sem=dot_recv_sem,
            device_id=partner(k),
            device_id_type=MESH,
        ).start()
    pltpu.make_async_copy(dots_recv, dots_recv, dot_recv_sem).wait()
    total = packed + jnp.sum(dots_recv[...], axis=0)

    for c in range(3):
        bb, bq, qq, qaq = [total[:, 4 * c + k : 4 * c + k + 1] for k in range(4)]
        step0 = bb / bq
        rr1 = step0 * step0 * qq - bb
        more = 1.0 + rr1 / bb
        curve = more * more * bq - 2.0 * more * step0 * qq + step0 * step0 * qaq
        step1 = rr1 / curve
        on_b = jnp.broadcast_to(step0 + step1 * more, (1, nr))
        on_q = jnp.broadcast_to(step1 * step0, (1, nr))
        part = slice(c * plane, (c + 1) * plane)
        out_ref[part, :] = on_b * bf[part, :] - on_q * qf[part, :]

    for _, _, copy in sent:
        copy.wait_send()
    pltpu.make_async_copy(dots_recv, dots_recv, dot_send_sem).wait()


def on_device(nd, ns, adjoint, base_flow, stiffness, mass_weight):
    _, nx, ny, nr = adjoint.shape
    rows = nx * ny
    blocks = np.kron(np.eye(nr // 8), TABLE)
    wd = jnp.asarray(split_weights(blocks.T))
    wt = jnp.asarray(split_weights(blocks))
    f32 = jnp.float32
    vmem = pl.BlockSpec(memory_space=pltpu.VMEM)
    hbm = pl.BlockSpec(memory_space=pltpu.HBM)
    out = pl.pallas_call(
        functools.partial(kernel, (nd, ns, nx, ny, nr)),
        out_shape=jax.ShapeDtypeStruct((3 * rows, nr), f32),
        in_specs=[hbm] * 6,
        out_specs=vmem,
        scratch_shapes=[
            pltpu.VMEM((3 * rows, nr), f32),
            pltpu.VMEM((3 * rows, nr), f32),
            pltpu.VMEM((rows, nr), f32),
            pltpu.VMEM((rows, nr), f32),
            pltpu.VMEM(wd.shape, wd.dtype),
            pltpu.VMEM(wt.shape, wt.dtype),
            pltpu.VMEM((3, rows, nr), f32),
            pltpu.VMEM((3, rows, nr), f32),
            pltpu.VMEM((3 * rows, nr), f32),
            pltpu.VMEM((3 * rows, nr), f32),
            pltpu.VMEM((3 * rows, nr), f32),
            pltpu.VMEM((2, 2, 3, nx, nr), f32),
            pltpu.VMEM((2, 4, 3, 1, nr), f32),
            pltpu.VMEM((2, 2, 3, ny, nr), f32),
            pltpu.VMEM((2, 2, 3, nx, nr), f32),
            pltpu.VMEM((2, 4, 3, 1, nr), f32),
            pltpu.VMEM((1, 1, nr), f32),
            pltpu.VMEM((nd * ns - 1, 1, nr), f32),
            pltpu.SemaphoreType.DMA((6,)),
            pltpu.SemaphoreType.DMA((2, len(GROUPS), 8)),
            pltpu.SemaphoreType.DMA((2, len(GROUPS), 8)),
            pltpu.SemaphoreType.DMA,
            pltpu.SemaphoreType.DMA,
        ],
        compiler_params=pltpu.CompilerParams(
            collective_id=0, has_side_effects=True, vmem_limit_bytes=VMEM_LIMIT
        ),
    )(
        adjoint.reshape(3 * rows, nr),
        base_flow.reshape(3 * rows, nr),
        stiffness.reshape(rows, nr),
        mass_weight.reshape(rows, nr),
        wd,
        wt,
    )
    return out.reshape(adjoint.shape)


def solution(mesh):
    in_specs = (
        P(None, "dom", "sub", None),
        P(None, "dom", "sub", None),
        P("dom", "sub", None),
        P("dom", "sub", None),
    )
    out_specs = P(None, "dom", "sub", None)
    return jax.shard_map(
        functools.partial(on_device, mesh.shape["dom"], mesh.shape["sub"]),
        mesh=mesh,
        in_specs=in_specs,
        out_specs=out_specs,
        check_vma=False,
    )
```

```python
import functools

import jax
import jax.numpy as jnp
import ml_dtypes
import numpy as np
from jax import lax
from jax.experimental import pallas as pl
from jax.experimental.pallas import tpu as pltpu
from jax.sharding import PartitionSpec as P

MESH = pl.DeviceIdType.MESH
shift_mass = 100.0
GROUPS = ((0, 1), (1, 1), (2, 1))
VMEM_LIMIT = 63 * 1024 * 1024

DIRECTIONS = ((1, 0), (-1, 0), (0, 1), (0, -1), (1, 1), (1, -1), (-1, 1), (-1, -1))


def legendre_seven(points):
    previous = np.ones(points.shape)
    current = points * 1.0
    for order in range(1, 7):
        following = ((2 * order + 1) * points * current - order * previous) / (order + 1)
        previous = current
        current = following
    return current


def derivative_table():
    degree = 7
    abscissae = np.array(
        [
            -1.0,
            -0.871740148509607,
            -0.591700181433142,
            -0.209299217902479,
            0.209299217902479,
            0.591700181433142,
            0.871740148509607,
            1.0,
        ]
    )
    legendre_values = legendre_seven(abscissae)
    deriv_table = np.zeros((degree + 1, degree + 1))
    for first_index in range(degree + 1):
        for second_index in range(degree + 1):
            if first_index != second_index:
                deriv_table[first_index, second_index] = legendre_values[first_index] / (
                    legendre_values[second_index]
                    * (abscissae[first_index] - abscissae[second_index])
                )
    deriv_table[0, 0] = -degree * (degree + 1) / 4.0
    deriv_table[degree, degree] = degree * (degree + 1) / 4.0
    return deriv_table


TABLE = derivative_table()


def apply_table(matrix, values):
    even = [values[j] + values[7 - j] for j in range(4)]
    odd = [values[j] - values[7 - j] for j in range(4)]
    result = [None] * 8
    for i in range(4):
        p = q = None
        for j in range(4):
            a = float((matrix[i, j] + matrix[i, 7 - j]) / 2)
            b = float((matrix[i, j] - matrix[i, 7 - j]) / 2)
            p = a * even[j] if p is None else p + a * even[j]
            q = b * odd[j] if q is None else q + b * odd[j]
        result[i] = q + p
        result[7 - i] = q - p
    return result


def split_weights(matrix):
    wide = matrix.astype(np.float32)
    high = wide.astype(ml_dtypes.bfloat16)
    low = (wide - high.astype(np.float32)).astype(high.dtype)
    return np.block([[high, low], [high, np.zeros_like(low)]])


def times_weights(rows, weights):
    high = rows.astype(jnp.bfloat16)
    low = (rows - high.astype(jnp.float32)).astype(jnp.bfloat16)
    both = jnp.concatenate([high, low], axis=1)
    product = jnp.dot(both, weights, preferred_element_type=jnp.float32)
    half = rows.shape[1]
    return product[:, :half] + product[:, half:]


def fold8(values):
    total = values[0:8]
    for start in range(8, values.shape[0], 8):
        total = total + values[start : start + 8]
    return total


def kernel(
    sizes,
    adjoint_hbm,
    base_hbm,
    stiff_hbm,
    mass_hbm,
    wd_hbm,
    wt_hbm,
    out_hbm,
    adj,
    base,
    stiff,
    mass,
    wd_ref,
    wt_ref,
    u0,
    u1,
    bf,
    qf,
    tmp,
    sy,
    sc,
    rx,
    ry,
    rc,
    dots_send,
    dots_recv,
    out_ref,
    load_sem,
    store_sem,
    send_sem,
    recv_sem,
    dot_send_sem,
    dot_recv_sem,
):
    nd, ns, nx, ny, nr = sizes
    plane = nx * ny
    me_d = lax.axis_index("dom")
    me_s = lax.axis_index("sub")

    loads = []
    for k, (src, dst) in enumerate(
        (
            (adjoint_hbm, adj),
            (base_hbm, base),
            (mass_hbm, mass),
            (wd_hbm, wd_ref),
            (stiff_hbm, stiff),
            (wt_hbm, wt_ref),
        )
    ):
        copy = pltpu.make_async_copy(src, dst, load_sem.at[k])
        copy.start()
        loads.append(copy)

    def flip(at, mask):
        bit, result = 1, at
        while bit <= mask:
            if mask & bit:
                result = result + bit * (1 - 2 * lax.rem(lax.div(at, bit), 2))
            bit *= 2
        return result

    def hops(k):
        return abs(k % ns) + bin(k // ns // 2).count("1")

    flips_d = [flip(me_d, k) for k in range(nd)]
    flips_s = [flip(me_s, k) for k in range(ns)]
    partners = sorted(range(1, nd * ns), key=hops, reverse=True)

    def partner(k):
        return (flips_d[k // ns], flips_s[k % ns])

    barrier = pltpu.get_barrier_semaphore()

    def greet(device):
        pl.semaphore_signal(barrier, inc=1, device_id=device, device_id_type=MESH)

    for k in partners:
        greet(partner(k))

    lane = lax.broadcasted_iota(jnp.int32, (1, nr), 1)
    inner = (lane > 0) & (lane < nr - 1)
    head = jnp.where((lane % 8 == 0) & inner, 1.0, 0.0)
    tail = jnp.where((lane % 8 == 7) & inner, 1.0, 0.0)
    wall = jnp.where(inner, 1.0, 0.0)
    lane_weight = wall / (1.0 + head + tail)

    def fold_lanes(v):
        v = v + tail * pltpu.roll(v, nr - 1, 1) + head * pltpu.roll(v, 1, 1)
        return v * wall

    def row(c, x):
        return slice(c * plane + x * ny, c * plane + (x + 1) * ny)

    def across(c, y):
        return pl.ds(c * plane + y, nx, stride=ny)

    def neighbour(k):
        dx, dy = DIRECTIONS[k]
        return (lax.rem(me_d + dx + nd, nd), lax.rem(me_s + dy + ns, ns))

    sent = []

    def send(p, c, u):
        for k in (2, 3):
            y = ny - 1 if k == 2 else 0
            buf = sy.at[p, k - 2, c]
            buf[...] = u[c, across(0, y), :]
            for e in range(8, nx, 8):
                lo = (e - 1) * ny + y
                hi = e * ny + y
                both = u[c, lo : lo + 1, :] + u[c, hi : hi + 1, :]
                buf[e - 1 : e, :] = both
                buf[e : e + 1, :] = both
        for k in range(4, 8):
            dx, dy = DIRECTIONS[k]
            at = ((nx - 1) * ny if dx > 0 else 0) + (ny - 1 if dy > 0 else 0)
            sc[p, k - 4, c] = u[c, at : at + 1, :]
        for g, (first, count) in enumerate(GROUPS):
            if c != first + count - 1:
                continue
            some = pl.ds(first, count)
            for k in (4, 5, 6, 7, 0, 1, 2, 3):
                dx, dy = DIRECTIONS[k]
                if dy == 0:
                    src = u.at[some, pl.ds((nx - 1) * ny if dx > 0 else 0, ny)]
                    dst = rx.at[p, k, some]
                elif dx == 0:
                    src, dst = sy.at[p, k - 2, some], ry.at[p, k - 2, some]
                else:
                    src, dst = sc.at[p, k - 4, some], rc.at[p, k - 4, some]
                copy = pltpu.make_async_remote_copy(
                    src_ref=src,
                    dst_ref=dst,
                    send_sem=send_sem.at[p, g, k],
                    recv_sem=recv_sem.at[p, g, k],
                    device_id=neighbour(k),
                    device_id_type=MESH,
                )
                copy.start()
                sent.append((p, first, copy))

    def assemble(p, c, u, dst):
        for phase, first, copy in sent:
            if phase == p and first == c:
                copy.wait_recv()
        for x in range(nx):
            if x == 0:
                v = u[c, row(0, 0), :] + rx[p, 0, c]
            elif x == nx - 1:
                v = u[c, row(0, x), :] + rx[p, 1, c]
            elif x % 8 == 7:
                v = u[c, row(0, x), :] + u[c, row(0, x + 1), :]
            elif x % 8 == 0:
                v = u[c, row(0, x), :] + u[c, row(0, x - 1), :]
            else:
                v = u[c, row(0, x), :]
            dst[row(c, x), :] = v
        for e in range(8, ny, 8):
            both = dst[across(c, e - 1), :] + dst[across(c, e), :]
            dst[across(c, e - 1), :] = both
            dst[across(c, e), :] = both
        dst[across(c, 0), :] = dst[across(c, 0), :] + ry[p, 0, c]
        dst[across(c, ny - 1), :] = dst[across(c, ny - 1), :] + ry[p, 1, c]
        for k in range(4, 8):
            dx, dy = DIRECTIONS[k]
            at = c * plane + (0 if dx > 0 else (nx - 1) * ny) + (0 if dy > 0 else ny - 1)
            dst[at : at + 1, :] = dst[at : at + 1, :] + rc[p, k - 4, c]

    def x_groups(c, ref):
        for xe in range(0, nx, 8):
            yield xe, [ref[row(c, xe + i), :] for i in range(8)]

    def y_groups(c, ref):
        for ye in range(0, ny, 8):
            yield ye, [ref[across(c, ye + j), :] for j in range(8)]

    for copy in loads[:4]:
        copy.wait()
    for c in range(3):
        part = slice(c * plane, (c + 1) * plane)
        for ye in range(0, ny, 8):
            grads = apply_table(TABLE, [adj[across(c, ye + j), :] for j in range(8)])
            terms = [base[across(1, ye + j), :] * grads[j] for j in range(8)]
            if c == 1:
                for d in range(3):
                    grads = apply_table(TABLE, [base[across(d, ye + j), :] for j in range(8)])
                    terms = [
                        terms[j] - adj[across(d, ye + j), :] * grads[j] for j in range(8)
                    ]
            for j in range(8):
                tmp[across(c, ye + j), :] = terms[j]
        radial = base[2 * plane : 3 * plane, :] * times_weights(adj[part, :], wd_ref[...])
        if c == 2:
            for d in range(3):
                some = slice(d * plane, (d + 1) * plane)
                radial = radial - adj[some, :] * times_weights(base[some, :], wd_ref[...])
        for xe in range(0, nx, 8):
            grads = apply_table(TABLE, [adj[row(c, xe + i), :] for i in range(8)])
            terms = [base[row(0, xe + i), :] * grads[i] for i in range(8)]
            if c == 0:
                for d in range(3):
                    grads = apply_table(TABLE, [base[row(d, xe + i), :] for i in range(8)])
                    terms = [terms[i] - adj[row(d, xe + i), :] * grads[i] for i in range(8)]
            for i in range(8):
                x = xe + i
                total = (
                    shift_mass * adj[row(c, x), :]
                    + terms[i]
                    + tmp[row(c, x), :]
                    + radial[x * ny : (x + 1) * ny]
                )
                u0[c, row(0, x), :] = fold_lanes(mass[row(0, x), :] * total)
        if c == 0:
            pl.semaphore_wait(barrier, nd * ns - 1)
        send(0, c, u0)

    for copy in loads[4:]:
        copy.wait()
    table_t = TABLE.T

    dots = [[None] * 4 for _ in range(3)]

    def add(c, k, values):
        values = fold8(values)
        dots[c][k] = values if dots[c][k] is None else dots[c][k] + values

    for c in range(3):
        part = slice(c * plane, (c + 1) * plane)
        assemble(0, c, u0, bf)
        radial = stiff[...] * times_weights(bf[part, :], wd_ref[...])
        radial = times_weights(radial, wt_ref[...])
        for ye, values in y_groups(c, bf):
            grads = apply_table(TABLE, values)
            terms = apply_table(
                table_t, [stiff[across(0, ye + j), :] * grads[j] for j in range(8)]
            )
            for j in range(8):
                tmp[across(c, ye + j), :] = terms[j]
        for xe, values in x_groups(c, bf):
            grads = apply_table(TABLE, values)
            terms = apply_table(
                table_t, [stiff[row(0, xe + i), :] * grads[i] for i in range(8)]
            )
            for i in range(8):
                x = xe + i
                total = (
                    shift_mass * mass[row(0, x), :] * values[i]
                    + terms[i]
                    + tmp[row(c, x), :]
                    + radial[x * ny : (x + 1) * ny]
                )
                total = fold_lanes(total)
                u1[c, row(0, x), :] = total
                add(c, 0, values[i] * u0[c, row(0, x), :])
                add(c, 1, values[i] * total)
        send(1, c, u1)

    for c in range(3):
        part = slice(c * plane, (c + 1) * plane)
        assemble(1, c, u1, qf)
        radial = times_weights(qf[part, :], wd_ref[...])
        add(c, 3, stiff[...] * radial * radial)
        for ye, values in y_groups(c, qf):
            grads = apply_table(TABLE, values)
            for j in range(8):
                add(c, 3, stiff[across(0, ye + j), :] * grads[j] * grads[j])
        for xe, values in x_groups(c, qf):
            grads = apply_table(TABLE, values)
            for i in range(8):
                x = xe + i
                add(c, 2, values[i] * u1[c, row(0, x), :])
                add(
                    c,
                    3,
                    stiff[row(0, x), :] * grads[i] * grads[i]
                    + shift_mass * mass[row(0, x), :] * values[i] * values[i],
                )

    packed = jnp.zeros((1, nr), jnp.float32)
    for c in range(3):
        for k in range(4):
            line = jnp.sum(dots[c][k], axis=0, keepdims=True)
            if k < 3:
                line = line * lane_weight
            packed = jnp.where(lane == 4 * c + k, jnp.sum(line, axis=1, keepdims=True), packed)
    dots_send[0] = packed
    for k in partners:
        pltpu.make_async_remote_copy(
            src_ref=dots_send.at[0],
            dst_ref=dots_recv.at[k - 1],
            send_sem=dot_send_sem,
            recv_sem=dot_recv_sem,
            device_id=partner(k),
            device_id_type=MESH,
        ).start()
    pltpu.make_async_copy(dots_recv, dots_recv, dot_recv_sem).wait()
    total = packed + jnp.sum(dots_recv[...], axis=0)

    stores = []
    for c in range(3):
        bb, bq, qq, qaq = [total[:, 4 * c + k : 4 * c + k + 1] for k in range(4)]
        step0 = bb / bq
        rr1 = step0 * step0 * qq - bb
        more = 1.0 + rr1 / bb
        curve = more * more * bq - 2.0 * more * step0 * qq + step0 * step0 * qaq
        step1 = rr1 / curve
        on_b = jnp.broadcast_to(step0 + step1 * more, (1, nr))
        on_q = jnp.broadcast_to(step1 * step0, (1, nr))
        part = slice(c * plane, (c + 1) * plane)
        out_ref[part, :] = on_b * bf[part, :] - on_q * qf[part, :]
        some = pl.ds(c * plane, plane)
        stores.append(
            pltpu.make_async_copy(out_ref.at[some], out_hbm.at[some], store_sem.at[c])
        )
        stores[-1].start()

    for _, _, copy in sent:
        copy.wait_send()
    for copy in stores:
        copy.wait()
    pltpu.make_async_copy(dots_recv, dots_recv, dot_send_sem).wait()


def on_device(nd, ns, adjoint, base_flow, stiffness, mass_weight):
    _, nx, ny, nr = adjoint.shape
    rows = nx * ny
    blocks = np.kron(np.eye(nr // 8), TABLE)
    wd = jnp.asarray(split_weights(blocks.T))
    wt = jnp.asarray(split_weights(blocks))
    f32 = jnp.float32
    hbm = pl.BlockSpec(memory_space=pltpu.HBM)
    out = pl.pallas_call(
        functools.partial(kernel, (nd, ns, nx, ny, nr)),
        out_shape=jax.ShapeDtypeStruct((3 * rows, nr), f32),
        in_specs=[hbm] * 6,
        out_specs=hbm,
        scratch_shapes=[
            pltpu.VMEM((3 * rows, nr), f32),
            pltpu.VMEM((3 * rows, nr), f32),
            pltpu.VMEM((rows, nr), f32),
            pltpu.VMEM((rows, nr), f32),
            pltpu.VMEM(wd.shape, wd.dtype),
            pltpu.VMEM(wt.shape, wt.dtype),
            pltpu.VMEM((3, rows, nr), f32),
            pltpu.VMEM((3, rows, nr), f32),
            pltpu.VMEM((3 * rows, nr), f32),
            pltpu.VMEM((3 * rows, nr), f32),
            pltpu.VMEM((3 * rows, nr), f32),
            pltpu.VMEM((2, 2, 3, nx, nr), f32),
            pltpu.VMEM((2, 4, 3, 1, nr), f32),
            pltpu.VMEM((2, 2, 3, ny, nr), f32),
            pltpu.VMEM((2, 2, 3, nx, nr), f32),
            pltpu.VMEM((2, 4, 3, 1, nr), f32),
            pltpu.VMEM((1, 1, nr), f32),
            pltpu.VMEM((nd * ns - 1, 1, nr), f32),
            pltpu.VMEM((3 * rows, nr), f32),
            pltpu.SemaphoreType.DMA((6,)),
            pltpu.SemaphoreType.DMA((3,)),
            pltpu.SemaphoreType.DMA((2, len(GROUPS), 8)),
            pltpu.SemaphoreType.DMA((2, len(GROUPS), 8)),
            pltpu.SemaphoreType.DMA,
            pltpu.SemaphoreType.DMA,
        ],
        compiler_params=pltpu.CompilerParams(
            collective_id=0, has_side_effects=True, vmem_limit_bytes=VMEM_LIMIT
        ),
    )(
        adjoint.reshape(3 * rows, nr),
        base_flow.reshape(3 * rows, nr),
        stiffness.reshape(rows, nr),
        mass_weight.reshape(rows, nr),
        wd,
        wt,
    )
    return out.reshape(adjoint.shape)


def solution(mesh):
    in_specs = (
        P(None, "dom", "sub", None),
        P(None, "dom", "sub", None),
        P("dom", "sub", None),
        P("dom", "sub", None),
    )
    out_specs = P(None, "dom", "sub", None)
    return jax.shard_map(
        functools.partial(on_device, mesh.shape["dom"], mesh.shape["sub"]),
        mesh=mesh,
        in_specs=in_specs,
        out_specs=out_specs,
        check_vma=False,
    )
```
